512 devices in a mesh: grp: 32 (over x, y, core), dev: 16 (over z).
Axes of the slice: x: 4, y: 4, z: 16, core: 2. Of those that a mesh axis runs over, the one named last changes fastest.
Arguments:
- embeddings: bfloat16 [262144, 768], P(('grp', 'dev')), may hold values from -64 to 64
- codeword_ids: int32 [262144, 96], P(('grp', 'dev')), may hold values from 0 to 255
Outputs:
- rotation: float32 [768, 768], P('dev')
- codebooks: float32 [96, 8, 256], replicated
The draws below stay inside these ranges and needn't reach their ends.
All inputs are finite; a program needn't handle non-finite values.
Results may differ from the reference program's by a relative error of at most 0.00065.
The reference program's roundings to bfloat16 on the way (of `recon`, `rotation_narrow` and `rotated`) count: a program that leaves them out, or rounds other values in their place, can miss the bound.
Values may be sent and summed in bfloat16 or wider, within the bound.
A program may use at most 64 MiB of HBM per device.

```python
import math
import jax
import jax.numpy as jnp
from jax import lax

D = 768
SUB = 96
K = 256
SUBW = 8
NS_STEPS = 5
ROWS = 262144


def shared_ids(key):
    return jax.random.randint(jax.random.fold_in(key, 11), (ROWS, SUB), 0, K).astype(jnp.int32)


def draw_codeword_ids(key, part):
    return shared_ids(key)


def draw_embeddings(key, part):
    ids_all = shared_ids(key)
    key = jax.random.fold_in(key, 2)
    centers = jnp.clip(jax.random.normal(jax.random.fold_in(key, 2), (SUB, K, SUBW), jnp.float32), -2.5, 2.5)
    noise = 0.5 * jnp.clip(jax.random.normal(jax.random.fold_in(key, 3), (ROWS, D), jnp.float32), -3.0, 3.0)
    factor = jnp.exp(jax.random.uniform(jax.random.fold_in(key, 4), (ROWS, 1), jnp.float32, math.log(0.5), math.log(2.0)))
    centers = centers - jnp.mean(centers, axis=1, keepdims=True)
    sub_index = jnp.arange(SUB, dtype=jnp.int32)[None, :]
    picked = centers[sub_index, ids_all].reshape(ROWS, D)
    mixed = picked + 0.25 * jnp.roll(picked, D // 2 + 3, axis=1)
    ramp = 1.0 + 2.0 * jnp.arange(ROWS, dtype=jnp.float32) / (ROWS - 1)
    return ((mixed + noise) * factor * ramp[:, None]).astype(jnp.bfloat16)


def setup_inputs(seed: int = 0) -> dict:
    streams_of = jax.random.split(jax.random.key(seed), 3)
    embeddings = draw_embeddings(jax.random.fold_in(streams_of[2], 71), 0)
    codeword_ids = draw_codeword_ids(jax.random.fold_in(streams_of[2], 71), 0)
    return {"embeddings": embeddings, "codeword_ids": codeword_ids}


def code_sums(field, codeword_ids):
    values = field.astype(jnp.float32).reshape(ROWS, SUB, SUBW).transpose(1, 0, 2)

    def per_subspace(members):
        ids_here, vals_here = members
        return jax.ops.segment_sum(vals_here, ids_here, num_segments=K)
    totals = lax.map(per_subspace, (codeword_ids.T, values))
    return totals.transpose(0, 2, 1)

def reference(embeddings, codeword_ids):
    ones_rows = jnp.ones((ROWS,), jnp.float32)
    counts = lax.map(lambda ids_here: jax.ops.segment_sum(ones_rows, ids_here, num_segments=K), codeword_ids.T)
    divisor = counts[:, None, :] + 1.0
    first_books = code_sums(embeddings, codeword_ids) / divisor
    narrow_books = first_books.astype(jnp.bfloat16).transpose(0, 2, 1)
    sub_index = jnp.arange(SUB, dtype=jnp.int32)[None, :]
    recon = narrow_books[sub_index, codeword_ids].reshape(ROWS, D)
    cross = lax.dot_general(embeddings, recon, (((0,), (0,)), ((), ())), preferred_element_type=jnp.float32)
    scale = 2.0 * jnp.sqrt((jnp.sum(cross * cross) + 1e-06) / D)
    polar = cross / scale
    for step_no in range(NS_STEPS):
        inner = jnp.dot(polar, polar.T, precision=lax.Precision.HIGHEST)
        polar = 1.5 * polar - 0.5 * jnp.dot(inner, polar, precision=lax.Precision.HIGHEST)
    rotation_narrow = polar.astype(jnp.bfloat16)
    rotated = jnp.dot(embeddings, rotation_narrow, preferred_element_type=jnp.float32).astype(jnp.bfloat16)
    codebooks = code_sums(rotated, codeword_ids) / divisor
    return (polar, codebooks)
```

```python
import functools

import jax
import jax.numpy as jnp
from jax import lax
from jax.experimental import pallas as pl
from jax.experimental.pallas import tpu as pltpu
from jax.sharding import PartitionSpec as P

K = 256
NS_STEPS = 5
LANES = 128
MESH = pl.DeviceIdType.MESH
TORUS = (4, 4)


def all_sum_kernel(
    nx, ny, nz, x_ref, out_ref,
    pair_buf, plane_buf, acc, z_src, z_buf, z_all,
    pair_sem, plane_sem, line_sem, line_back_sem, plane_back_sem, pair_back_sem, send_sem,
):
    planes = nx * ny
    rows, cols = x_ref.shape
    half, part = rows // 2, rows // (2 * planes)
    lane_tiles = cols // LANES
    per_z = part * lane_tiles // nz
    grp, z = lax.axis_index("grp"), lax.axis_index("dev")
    core, xy = lax.rem(grp, 2), lax.div(grp, 2)
    x, y = lax.div(xy, ny), lax.rem(xy, ny)

    def ahead(i):
        return lax.rem(x + lax.div(i, ny), nx) * ny + lax.rem(y + lax.rem(i, ny), ny)

    def behind(i):
        return lax.rem(x + nx - lax.div(i, ny), nx) * ny + lax.rem(y + ny - lax.rem(i, ny), ny)

    def sibling():
        return {"grp": xy * 2 + 1 - core, "dev": z}

    def in_plane(g):
        return {"grp": g * 2 + core, "dev": z}

    def in_line(i):
        return {"grp": grp, "dev": lax.rem(z + i, nz)}

    def chunk(which_core, g):
        return pl.ds(pl.multiple_of(which_core * half + g * part, 8), part)

    def piece(g):
        return pl.ds(pl.multiple_of(g * part, 8), part)

    def copy(src, dst, send, recv, device):
        return pltpu.make_async_remote_copy(
            src_ref=src, dst_ref=dst, send_sem=send, recv_sem=recv,
            device_id=device, device_id_type=MESH,
        )

    barrier = pltpu.get_barrier_semaphore()
    pl.semaphore_signal(barrier, inc=1, device_id=sibling(), device_id_type=MESH)

    @pl.loop(1, planes)
    def _(i):
        pl.semaphore_signal(barrier, inc=1, device_id=in_plane(ahead(i)), device_id_type=MESH)

    @pl.loop(1, nz)
    def _(i):
        pl.semaphore_signal(barrier, inc=1, device_id=in_line(i), device_id_type=MESH)

    pl.semaphore_wait(barrier, 1 + planes - 1 + nz - 1)

    def pair_copy(i):
        g = ahead(lax.rem(i, planes))
        return copy(
            x_ref.at[chunk(1 - core, g)], pair_buf.at[piece(g)],
            send_sem.at[0], pair_sem.at[lax.rem(i, planes)], sibling(),
        )

    @pl.loop(1, planes + 1)
    def _(i):
        pair_copy(i).start()

    def plane_copy(i):
        g = ahead(i)
        return copy(
            pair_buf.at[piece(g)], plane_buf.at[i - 1],
            send_sem.at[1], plane_sem.at[i - 1], in_plane(g),
        )

    @pl.loop(1, planes)
    def _(i):
        pair_copy(i).wait_recv()
        g = ahead(i)
        pair_buf[piece(g)] = pair_buf[piece(g)] + x_ref[chunk(core, g)]
        plane_copy(i).start()

    pair_copy(planes).wait_recv()
    acc[...] = pair_buf[piece(xy)] + x_ref[chunk(core, xy)]

    @pl.loop(1, planes)
    def _(i):
        plane_copy(i).wait_recv()
        acc[...] += plane_buf[i - 1]

    for s in range(part):
        for l in range(lane_tiles):
            r = s * lane_tiles + l
            z_src[r // per_z, r % per_z] = acc[s : s + 1, l * LANES : (l + 1) * LANES]

    def line_copy(i):
        return copy(
            z_src.at[lax.rem(z + i, nz)], z_buf.at[i - 1],
            send_sem.at[2], line_sem.at[i - 1], in_line(i),
        )

    def line_back_copy(i):
        return copy(
            z_all.at[z], z_all.at[z], send_sem.at[3], line_back_sem.at[i - 1], in_line(i),
        )

    @pl.loop(1, nz)
    def _(i):
        line_copy(i).start()

    z_all[z] = z_src[z]

    @pl.loop(1, nz)
    def _(i):
        line_copy(i).wait_recv()
        z_all[z] += z_buf[i - 1]

    @pl.loop(1, nz)
    def _(i):
        line_back_copy(i).start()

    def line_back_arrival(i):
        landed = z_all.at[lax.rem(z + nz - i, nz)]
        return copy(landed, landed, send_sem.at[3], line_back_sem.at[i - 1], in_line(i))

    @pl.loop(1, nz)
    def _(i):
        line_back_arrival(i).wait_recv()

    for s in range(part):
        for l in range(lane_tiles):
            r = s * lane_tiles + l
            acc[s : s + 1, l * LANES : (l + 1) * LANES] = z_all[r // per_z, r % per_z]
    out_ref[chunk(core, xy)] = acc[...]

    def plane_back_copy(i, g, device):
        block = out_ref.at[chunk(core, g)]
        return copy(block, block, send_sem.at[4], plane_back_sem.at[i - 1], device)

    def pair_back_copy(i, which_core):
        block = out_ref.at[chunk(which_core, behind(i))]
        return copy(block, block, send_sem.at[5], pair_back_sem.at[i], sibling())

    @pl.loop(1, planes)
    def _(i):
        plane_back_copy(i, xy, in_plane(ahead(i))).start()

    pair_back_copy(0, core).start()

    @pl.loop(1, planes)
    def _(i):
        plane_back_copy(i, behind(i), in_plane(ahead(i))).wait_recv()
        pair_back_copy(i, core).start()

    @pl.loop(0, planes)
    def _(i):
        pair_back_copy(i, 1 - core).wait_recv()

    def drain(like, k):
        pltpu.make_async_copy(like, like, send_sem.at[k]).wait()

    drain(pair_buf, 0)
    drain(plane_buf, 1)
    drain(z_buf, 2)
    drain(z_buf, 3)
    drain(plane_buf, 4)
    drain(pair_buf, 5)


def all_sum(x, collective_id, nz, torus=TORUS):
    nx, ny = torus
    planes = nx * ny
    rows, cols = x.shape
    part = rows // (2 * planes)
    per_z = part * cols // LANES // nz
    dma = pltpu.SemaphoreType.DMA
    return pl.pallas_call(
        functools.partial(all_sum_kernel, nx, ny, nz),
        out_shape=jax.ShapeDtypeStruct((rows, cols), jnp.float32),
        in_specs=[pl.BlockSpec(memory_space=pltpu.VMEM)],
        out_specs=pl.BlockSpec(memory_space=pltpu.VMEM),
        scratch_shapes=[
            pltpu.VMEM((rows // 2, cols), jnp.float32),
            pltpu.VMEM((planes - 1, part, cols), jnp.float32),
            pltpu.VMEM((part, cols), jnp.float32),
            pltpu.VMEM((nz, per_z, 1, LANES), jnp.float32),
            pltpu.VMEM((nz - 1, per_z, 1, LANES), jnp.float32),
            pltpu.VMEM((nz, per_z, 1, LANES), jnp.float32),
            dma((planes,)),
            dma((planes - 1,)),
            dma((nz - 1,)),
            dma((nz - 1,)),
            dma((planes - 1,)),
            dma((planes,)),
            dma((6,)),
        ],
        compiler_params=pltpu.CompilerParams(
            collective_id=collective_id, has_side_effects=True, vmem_limit_bytes=40 << 20
        ),
        cost_estimate=pl.CostEstimate(
            flops=2 * rows * cols, bytes_accessed=8 * rows * cols, transcendentals=0
        ),
    )(x)


def split(value):
    hi = value.astype(jnp.bfloat16)
    return hi, (value - hi.astype(jnp.float32)).astype(jnp.bfloat16)


def polar_kernel(cross_ref, out_ref, p_hi, p_lo, g_hi, g_lo):
    width = cross_ref.shape[0]
    tile = 256
    cross = cross_ref[...]
    total = jnp.sum(cross * cross, keepdims=True)
    out_ref[...] = cross / (2.0 * jnp.sqrt((total + 1e-06) / width))

    def times(a, b_hi, b_lo, dims):
        dot = functools.partial(
            lax.dot_general, dimension_numbers=(dims, ((), ())), preferred_element_type=jnp.float32
        )
        return dot(a[0], b_hi) + (dot(a[0], b_lo) + dot(a[1], b_hi))

    @pl.loop(0, NS_STEPS)
    def _(step):
        hi, lo = split(out_ref[...])
        p_hi[...] = hi
        p_lo[...] = lo
        for r in range(0, width, tile):
            band = slice(r, r + tile)
            gram = times((p_hi[band], p_lo[band]), p_hi[...], p_lo[...], ((1,), (1,)))
            hi, lo = split(gram)
            g_hi[band] = hi
            g_lo[band] = lo
        for r in range(0, width, tile):
            band = slice(r, r + tile)
            cubic = times((g_hi[band], g_lo[band]), p_hi[...], p_lo[...], ((1,), (0,)))
            out_ref[band] = 1.5 * out_ref[band] - 0.5 * cubic


def polar_factor(cross):
    width = cross.shape[0]
    return pl.pallas_call(
        polar_kernel,
        out_shape=jax.ShapeDtypeStruct((width, width), jnp.float32),
        in_specs=[pl.BlockSpec(memory_space=pltpu.VMEM)],
        out_specs=pl.BlockSpec(memory_space=pltpu.VMEM),
        scratch_shapes=[pltpu.VMEM((width, width), jnp.bfloat16)] * 4,
        compiler_params=pltpu.CompilerParams(vmem_limit_bytes=40 << 20),
        cost_estimate=pl.CostEstimate(
            flops=60 * width**3, bytes_accessed=8 * width * width, transcendentals=0
        ),
    )(cross)


def onehot_rows(ids_group):
    return (ids_group[:, :, None] == jnp.arange(K, dtype=jnp.int32)[None, None, :]).astype(
        jnp.bfloat16
    )


def group_layout(field, groups):
    rows_local = field.shape[0]
    return field.reshape(rows_local, groups, field.shape[1] // groups).transpose(1, 0, 2)


def group_sums(field, grouped_ids, sub_width, want_counts):
    rows_local = field.shape[0]
    groups = grouped_ids.shape[0]

    def per_group(members):
        ids_group, field_group = members
        selector = onehot_rows(ids_group)
        values = field_group.reshape(rows_local, 8, sub_width)
        totals = jnp.einsum("rmj,rmk->mjk", values, selector, preferred_element_type=jnp.float32)
        if want_counts:
            return (totals, jnp.sum(selector, axis=0, dtype=jnp.float32))
        return totals

    outcome = lax.map(per_group, (grouped_ids, group_layout(field, groups)))
    if want_counts:
        return (outcome[0].reshape(groups * 8, sub_width, K), outcome[1].reshape(groups * 8, K))
    return outcome.reshape(groups * 8, sub_width, K)


def on_device(embeddings, codeword_ids):
    rows_local, width = embeddings.shape
    subspaces = codeword_ids.shape[1]
    sub_width = width // subspaces
    groups = subspaces // 8
    grouped_ids = codeword_ids.reshape(rows_local, groups, 8).transpose(1, 0, 2)
    code_totals, code_counts = group_sums(embeddings, grouped_ids, sub_width, True)
    nz = lax.axis_size("dev")
    summed = all_sum(
        jnp.concatenate([code_totals.reshape(subspaces * sub_width, K),
                         code_counts, jnp.zeros((160, K), jnp.float32)]), 1, nz)
    code_totals = summed[:width].reshape(subspaces, sub_width, K)
    code_counts = summed[width : width + subspaces]
    divisor = code_counts[:, None, :] + 1.0
    first_books = (code_totals / divisor).astype(jnp.bfloat16)

    def rebuild(members):
        ids_group, books_group = members
        selector = onehot_rows(ids_group)
        rebuilt = jnp.einsum(
            "rmk,mjk->rmj", selector, books_group, preferred_element_type=jnp.float32
        )
        return rebuilt.astype(jnp.bfloat16).reshape(rows_local, 8 * sub_width)

    recon_groups = lax.map(rebuild, (grouped_ids, first_books.reshape(groups, 8, sub_width, K)))
    recon = recon_groups.transpose(1, 0, 2).reshape(rows_local, width)
    partial_cross = lax.dot_general(
        embeddings, recon, (((0,), (0,)), ((), ())), preferred_element_type=jnp.float32
    )
    share = width // lax.axis_size("dev")
    rotation_full = polar_factor(all_sum(partial_cross, 2, nz))
    own_rows = lax.dynamic_slice_in_dim(rotation_full, lax.axis_index("dev") * share, share, 0)
    rotated = jnp.dot(
        embeddings, rotation_full.astype(jnp.bfloat16), preferred_element_type=jnp.float32
    ).astype(jnp.bfloat16)
    rotated_totals = group_sums(rotated, grouped_ids, sub_width, False)
    rotated_totals = all_sum(rotated_totals.reshape(width, K), 3, nz)
    return (own_rows, rotated_totals.reshape(subspaces, sub_width, K) / divisor)


def solution(mesh):
    return jax.shard_map(
        on_device,
        mesh=mesh,
        in_specs=(P(("grp", "dev"), None), P(("grp", "dev"), None)),
        out_specs=(P("dev", None), P()),
        check_vma=False,
    )
```

```python
import functools

import jax
import jax.numpy as jnp
from jax import lax
from jax.experimental import pallas as pl
from jax.experimental.pallas import tpu as pltpu
from jax.sharding import PartitionSpec as P

K = 256
NS_STEPS = 5
LANES = 128
MESH = pl.DeviceIdType.MESH
TORUS = (4, 4)
SUBW = 8
FIRST_CHUNKS = 4
CROSS_CHUNKS = 3
LAST_CHUNKS = 3
CHUNK = 256


class Place:
    def __init__(self, nx, ny, nz):
        self.nx, self.ny, self.nz, self.planes = nx, ny, nz, nx * ny
        self.grp, self.z = lax.axis_index("grp"), lax.axis_index("dev")
        self.core, self.xy = lax.rem(self.grp, 2), lax.div(self.grp, 2)
        self.x, self.y = lax.div(self.xy, ny), lax.rem(self.xy, ny)

    def sibling(self):
        return {"grp": self.xy * 2 + 1 - self.core, "dev": self.z}

    def plane_partner(self, i):
        nx, ny = self.nx, self.ny
        own = (nx - nx // 2) % nx * ny + (ny - ny // 2) % ny
        i = jnp.where(i >= own, i + 1, i)
        dx, dy = nx // 2 + lax.div(i, ny), ny // 2 + lax.rem(i, ny)
        return lax.rem(self.x + dx, nx) * ny + lax.rem(self.y + dy, ny)

    def in_plane(self, g):
        return {"grp": g * 2 + self.core, "dev": self.z}

    def line_partner(self, i):
        offset = self.nz // 2 + lax.div(i, 2) * (2 * lax.rem(i, 2) - 1)
        return lax.rem(self.z + offset, self.nz)

    def in_line(self, z):
        return {"grp": self.grp, "dev": z}

    def greet(self):
        barrier = pltpu.get_barrier_semaphore()

        def signal(device):
            pl.semaphore_signal(barrier, inc=1, device_id=device, device_id_type=MESH)

        signal(self.sibling())

        @pl.loop(0, self.planes - 1)
        def _(i):
            signal(self.in_plane(self.plane_partner(i)))

        @pl.loop(1, self.nz)
        def _(i):
            signal(self.in_line(self.line_partner(i)))

    def meet(self):
        pl.semaphore_wait(pltpu.get_barrier_semaphore(), 1 + self.planes - 1 + self.nz - 1)


def remote(src, dst, send, recv, device):
    return pltpu.make_async_remote_copy(
        src_ref=src, dst_ref=dst, send_sem=send, recv_sem=recv,
        device_id=device, device_id_type=MESH,
    )


def await_bytes(like, sem):
    pltpu.make_async_copy(like, like, sem).wait()


class AllSum:
    def __init__(self, place, refs):
        self.at = place
        (self.x, self.out, self.pair_buf, self.plane_buf, self.acc, self.z_src, self.z_buf,
         self.z_all, self.recv, self.send) = refs
        self.chunks, self.half, self.cols = self.pair_buf.shape
        self.part = self.half // place.planes
        self.lane_tiles = self.cols // LANES
        self.per_z = self.part * self.lane_tiles // place.nz

    def part_rows(self, c, core, g):
        return pl.ds(pl.multiple_of((2 * c + core) * self.half + g * self.part, 8), self.part)

    def half_rows(self, c, core):
        return pl.ds(pl.multiple_of((2 * c + core) * self.half, 8), self.half)

    def pair(self, c):
        at = self.at
        remote(
            self.x.at[self.half_rows(c, 1 - at.core)], self.pair_buf.at[c],
            self.send.at[0], self.recv.at[0, c], at.sibling(),
        ).start()

    def plane(self, c):
        at = self.at
        await_bytes(self.pair_buf.at[c], self.recv.at[0, c])
        self.pair_buf[c] = self.pair_buf[c] + self.x[self.half_rows(c, at.core)]

        @pl.loop(0, at.planes - 1)
        def _(i):
            g = at.plane_partner(i)
            rows = pl.ds(pl.multiple_of(g * self.part, 8), self.part)
            remote(
                self.pair_buf.at[c, rows], self.plane_buf.at[c, i],
                self.send.at[1], self.recv.at[1, c], at.in_plane(g),
            ).start()

    def line(self, c):
        at = self.at
        await_bytes(self.plane_buf.at[c], self.recv.at[1, c])
        rows = pl.ds(pl.multiple_of(at.xy * self.part, 8), self.part)
        total = self.pair_buf[c, rows]
        for i in range(at.planes - 1):
            total = total + self.plane_buf[c, i]
        self.acc[...] = total
        for s in range(self.part):
            for l in range(self.lane_tiles):
                r = s * self.lane_tiles + l
                self.z_src[c, r // self.per_z, r % self.per_z] = self.acc[
                    s : s + 1, l * LANES : (l + 1) * LANES
                ]

        @pl.loop(1, at.nz)
        def _(i):
            z = at.line_partner(i)
            remote(
                self.z_src.at[c, z], self.z_buf.at[c, i - 1],
                self.send.at[2], self.recv.at[2, c], at.in_line(z),
            ).start()

    def line_back(self, c):
        at = self.at
        await_bytes(self.z_buf.at[c], self.recv.at[2, c])
        total = self.z_src[c, at.z]
        for i in range(at.nz - 1):
            total = total + self.z_buf[c, i]
        self.z_all[c, at.z] = total

        @pl.loop(1, at.nz)
        def _(i):
            z = at.line_partner(i)
            block = self.z_all.at[c, at.z]
            remote(block, block, self.send.at[3], self.recv.at[3, c], at.in_line(z)).start()

    def plane_back(self, c):
        at = self.at
        await_bytes(self.z_buf.at[c], self.recv.at[3, c])
        for s in range(self.part):
            for l in range(self.lane_tiles):
                r = s * self.lane_tiles + l
                self.acc[s : s + 1, l * LANES : (l + 1) * LANES] = self.z_all[
                    c, r // self.per_z, r % self.per_z
                ]
        own = self.part_rows(c, at.core, at.xy)
        self.out[own] = self.acc[...]

        @pl.loop(0, at.planes - 1)
        def _(i):
            block = self.out.at[own]
            remote(
                block, block, self.send.at[4], self.recv.at[4, c],
                at.in_plane(at.plane_partner(i)),
            ).start()

    def pair_back(self, c):
        at = self.at
        await_bytes(self.plane_buf.at[c], self.recv.at[4, c])
        block = self.out.at[self.half_rows(c, at.core)]
        remote(block, block, self.send.at[5], self.recv.at[5, c], at.sibling()).start()

    def arrive(self, c):
        await_bytes(self.pair_buf.at[c], self.recv.at[5, c])

    def drain(self):
        for k, like in enumerate(
            (self.pair_buf, self.plane_buf, self.z_buf, self.z_buf, self.plane_buf, self.pair_buf)
        ):
            await_bytes(like, self.send.at[k])


def all_sum_scratch(chunks, rows, cols, nx, ny, nz):
    planes = nx * ny
    part = rows // (2 * planes)
    per_z = part * (cols // LANES) // nz
    return [
        pltpu.VMEM((chunks * rows, cols), jnp.float32),
        pltpu.VMEM((chunks * rows, cols), jnp.float32),
        pltpu.VMEM((chunks, rows // 2, cols), jnp.float32),
        pltpu.VMEM((chunks, planes - 1, part, cols), jnp.float32),
        pltpu.VMEM((part, cols), jnp.float32),
        pltpu.VMEM((chunks, nz, per_z, 1, LANES), jnp.float32),
        pltpu.VMEM((chunks, nz - 1, per_z, 1, LANES), jnp.float32),
        pltpu.VMEM((chunks, nz, per_z, 1, LANES), jnp.float32),
        pltpu.SemaphoreType.DMA((6, chunks)),
        pltpu.SemaphoreType.DMA((6,)),
    ]


def split(value):
    hi = value.astype(jnp.bfloat16)
    return hi, (value - hi.astype(jnp.float32)).astype(jnp.bfloat16)


def dot(a, b, dims):
    return lax.dot_general(
        a, b, dimension_numbers=(dims, ((), ())), preferred_element_type=jnp.float32
    )


def newton_schulz(cross, q, p_hi, p_lo, g_hi, g_lo):
    width = q.shape[0]
    tile = 256
    total = jnp.sum(cross[...] * cross[...], keepdims=True)
    q[...] = cross[...] / (2.0 * jnp.sqrt((total + 1e-06) / width))

    def times(a, b_hi, b_lo, dims):
        return dot(a[0], b_hi, dims) + (dot(a[0], b_lo, dims) + dot(a[1], b_hi, dims))

    @pl.loop(0, NS_STEPS)
    def _(step):
        hi, lo = split(q[...])
        p_hi[...] = hi
        p_lo[...] = lo
        for r in range(0, width, tile):
            band = slice(r, r + tile)
            gram = times((p_hi[band], p_lo[band]), p_hi[...], p_lo[...], ((1,), (1,)))
            hi, lo = split(gram)
            g_hi[band] = hi
            g_lo[band] = lo
        for r in range(0, width, tile):
            band = slice(r, r + tile)
            cubic = times((g_hi[band], g_lo[band]), p_hi[...], p_lo[...], ((1,), (0,)))
            q[band] = 1.5 * q[band] - 0.5 * cubic


def kernel(
    nx, ny, nz, emb, emb_t, ids_t, rot_out, books_out,
    *scratch,
):
    first_refs, cross_refs, last_refs = scratch[0:10], scratch[10:20], scratch[20:30]
    books, recon_t, counts, p_hi, p_lo, g_hi, g_lo, polar, rot, rot_t = scratch[30:]
    rows = emb.shape[0]
    width = emb.shape[1]
    place = Place(nx, ny, nz)
    place.greet()
    first = AllSum(place, first_refs)
    cross = AllSum(place, cross_refs)
    last = AllSum(place, last_refs)
    subs = 24
    top = lax.broadcasted_iota(jnp.int32, (2 * SUBW, rows), 0) < SUBW
    first_eight = lax.broadcasted_iota(jnp.int32, (2 * SUBW, K), 0) < SUBW
    codes = lax.broadcasted_iota(jnp.int32, (K, rows), 0).astype(jnp.float32).astype(jnp.bfloat16)
    one, zero = jnp.array(1, jnp.bfloat16), jnp.array(0, jnp.bfloat16)

    def selector(m):
        return jnp.where(ids_t[pl.ds(m, 1), :].astype(jnp.bfloat16) == codes, one, zero)

    def pair_rows(m):
        return pl.ds(pl.multiple_of(m * SUBW, 16), 2 * SUBW)

    def first_sums(t):
        base = t * CHUNK

        @pl.loop(0, subs // 8)
        def _(u):
            for s in range(0, 8, 2):
                m = u * 8 + s
                values = emb_t[pair_rows(t * subs + m), :]
                both = dot(jnp.where(top, values, one), selector(t * subs + m), ((1,), (1,)))
                at = pl.ds(pl.multiple_of(base + m * SUBW, 8), SUBW)
                first.x[at, :] = both[:SUBW]
                first.x[pl.ds(base + subs * SUBW + m, 1), :] = both[SUBW : SUBW + 1]
                both = dot(jnp.where(top, one, values), selector(t * subs + m + 1), ((1,), (1,)))
                at = pl.ds(pl.multiple_of(base + m * SUBW + SUBW, 8), SUBW)
                first.x[at, :] = both[SUBW:]
                first.x[pl.ds(base + subs * SUBW + m + 1, 1), :] = both[:1]

        used = subs * (SUBW + 1)
        first.x[base + used : base + CHUNK, :] = jnp.zeros((CHUNK - used, K), jnp.float32)

    def first_books(t):
        base = t * CHUNK
        tally = base + subs * SUBW
        counts[t * subs : (t + 1) * subs, :] = first.out[tally : tally + subs, :] + 1.0
        for m in range(0, subs, 2):
            g = t * subs + m
            divisor = jnp.where(first_eight, counts[g : g + 1, :], counts[g + 1 : g + 2, :])
            sums = first.out[base + m * SUBW : base + (m + 2) * SUBW, :]
            books[g * SUBW : (g + 2) * SUBW, :] = (sums / divisor).astype(jnp.bfloat16)

        @pl.loop(0, subs // 8)
        def _(u):
            for s in range(0, 8, 2):
                m = t * subs + u * 8 + s
                book = books[pair_rows(m), :]
                even = dot(book, selector(m), ((1,), (0,)))
                odd = dot(book, selector(m + 1), ((1,), (0,)))
                recon_t[pair_rows(m), :] = jnp.where(top, even, odd).astype(jnp.bfloat16)

    def cross_rows(j):
        band = slice(j * CHUNK, (j + 1) * CHUNK)
        cross.x[band, :] = dot(recon_t[band, :], emb[...], ((1,), (0,)))

    def last_sums(j):
        band = slice(j * CHUNK, (j + 1) * CHUNK)
        rot_t[...] = dot(p_hi[band, :], emb_t[...], ((1,), (0,))).astype(jnp.bfloat16)

        @pl.loop(0, CHUNK // SUBW // 8)
        def _(u):
            for s in range(0, 8, 2):
                m = u * 8 + s
                values = rot_t[pair_rows(m), :]
                base = j * CHUNK // SUBW
                even = dot(values, selector(base + m), ((1,), (1,)))
                odd = dot(values, selector(base + m + 1), ((1,), (1,)))
                at = pl.ds(pl.multiple_of(j * CHUNK + m * SUBW, 8), SUBW)
                last.x[at, :] = even[:SUBW]
                at = pl.ds(pl.multiple_of(j * CHUNK + m * SUBW + SUBW, 8), SUBW)
                last.x[at, :] = odd[SUBW:]

    first_sums(0)
    place.meet()
    first.pair(0)
    first_sums(1)
    first.pair(1)
    first.plane(0)
    first_sums(2)
    first.pair(2)
    first.plane(1)
    first_sums(3)
    first.pair(3)
    first.plane(2)
    first.line(0)
    first.plane(3)
    for t in range(1, FIRST_CHUNKS):
        first.line(t)
    for t in range(FIRST_CHUNKS):
        first.line_back(t)
    for t in range(FIRST_CHUNKS):
        first.plane_back(t)
    first.pair_back(0)
    first.pair_back(1)
    first.arrive(0)
    first_books(0)
    first.pair_back(2)
    first.arrive(1)
    first_books(1)
    cross_rows(0)
    cross.pair(0)
    first.pair_back(3)
    first.arrive(2)
    first_books(2)
    cross_rows(1)
    cross.pair(1)
    cross.plane(0)
    first.arrive(3)
    first_books(3)
    cross_rows(2)
    cross.pair(2)
    cross.plane(1)
    cross.line(0)
    cross.plane(2)
    cross.line(1)
    cross.line(2)
    for stage in (cross.line_back, cross.plane_back, cross.pair_back, cross.arrive):
        for t in range(CROSS_CHUNKS):
            stage(t)

    newton_schulz(cross.out, polar, p_hi, p_lo, g_hi, g_lo)
    p_hi[...] = polar[...].astype(jnp.bfloat16)
    last_sums(0)
    last.pair(0)
    last_sums(1)
    last.pair(1)
    last.plane(0)
    last_sums(2)
    last.pair(2)
    last.plane(1)
    last.line(0)
    last.plane(2)
    last.line(1)
    last.line(2)
    rot[...] = polar[...].T
    share = width // nz
    rot_out[...] = rot[pl.ds(pl.multiple_of(place.z * share, 8), share), :]
    for stage in (last.line_back, last.plane_back, last.pair_back):
        for t in range(LAST_CHUNKS):
            stage(t)
    for t in range(LAST_CHUNKS):
        last.arrive(t)
        for m in range(t * CHUNK // SUBW, (t + 1) * CHUNK // SUBW):
            at = slice(m * SUBW, (m + 1) * SUBW)
            books_out[at, :] = last.out[at, :] / counts[m : m + 1, :]
    first.drain()
    cross.drain()
    last.drain()


def on_device(nz, torus, embeddings, codeword_ids):
    nx, ny = torus
    rows, width = embeddings.shape
    vmem = pl.BlockSpec(memory_space=pltpu.VMEM)
    bf16 = jnp.bfloat16
    square = pltpu.VMEM((width, width), bf16)
    subspaces = codeword_ids.shape[1]
    rotation, books = pl.pallas_call(
        functools.partial(kernel, nx, ny, nz),
        out_shape=(
            jax.ShapeDtypeStruct((width // nz, width), jnp.float32),
            jax.ShapeDtypeStruct((width, K), jnp.float32),
        ),
        in_specs=[vmem] * 3,
        out_specs=(vmem, vmem),
        scratch_shapes=[
            *all_sum_scratch(FIRST_CHUNKS, CHUNK, K, nx, ny, nz),
            *all_sum_scratch(CROSS_CHUNKS, CHUNK, width, nx, ny, nz),
            *all_sum_scratch(LAST_CHUNKS, CHUNK, K, nx, ny, nz),
            pltpu.VMEM((width, K), bf16),
            pltpu.VMEM((width, rows), bf16),
            pltpu.VMEM((subspaces, K), jnp.float32),
            square, square, square, square,
            pltpu.VMEM((width, width), jnp.float32),
            pltpu.VMEM((width, width), jnp.float32),
            pltpu.VMEM((CHUNK, rows), bf16),
        ],
        compiler_params=pltpu.CompilerParams(
            collective_id=1, has_side_effects=True, vmem_limit_bytes=56 << 20
        ),
        cost_estimate=pl.CostEstimate(
            flops=60 * width**3, bytes_accessed=8 * width * width, transcendentals=0
        ),
    )(embeddings, embeddings.T, codeword_ids.T.astype(jnp.float32))
    return rotation, books.reshape(subspaces, SUBW, K)


def solution(mesh, torus=TORUS):
    return jax.shard_map(
        functools.partial(on_device, mesh.shape["dev"], torus),
        mesh=mesh,
        in_specs=(P(("grp", "dev"), None), P(("grp", "dev"), None)),
        out_specs=(P("dev", None), P()),
        check_vma=False,
    )
```

```python
import functools

import jax
import jax.numpy as jnp
from jax import lax
from jax.experimental import pallas as pl
from jax.experimental.pallas import tpu as pltpu
from jax.sharding import PartitionSpec as P

K = 256
NS_STEPS = 5
LANES = 128
MESH = pl.DeviceIdType.MESH
TORUS = (4, 4)
SUBW = 8
FIRST_CHUNKS = 4
CROSS_CHUNKS = 3
LAST_CHUNKS = 3
CHUNK = 256


def line_shape(nz):
    members = 4 if nz % 16 == 0 else nz // 2
    return members, nz // members


class Place:
    def __init__(self, nx, ny, nz):
        self.nx, self.ny, self.nz, self.planes = nx, ny, nz, nx * ny
        self.grp, self.z = lax.axis_index("grp"), lax.axis_index("dev")
        self.core, self.xy = lax.rem(self.grp, 2), lax.div(self.grp, 2)
        self.x, self.y = lax.div(self.xy, ny), lax.rem(self.xy, ny)
        self.members, self.runs = line_shape(nz)
        self.run, self.member = lax.div(self.z, self.members), lax.rem(self.z, self.members)

    def sibling(self):
        return {"grp": self.xy * 2 + 1 - self.core, "dev": self.z}

    def plane_partner(self, i):
        nx, ny = self.nx, self.ny
        own = (nx - nx // 2) % nx * ny + (ny - ny // 2) % ny
        i = jnp.where(i >= own, i + 1, i)
        dx, dy = nx // 2 + lax.div(i, ny), ny // 2 + lax.rem(i, ny)
        return lax.rem(self.x + dx, nx) * ny + lax.rem(self.y + dy, ny)

    def in_plane(self, g):
        return {"grp": g * 2 + self.core, "dev": self.z}

    def member_partner(self, i):
        return lax.rem(self.member + i, self.members)

    def run_partner(self, i):
        return lax.rem(self.run + i, self.runs)

    def in_run(self, member):
        return self.in_line(self.run * self.members + member)

    def across_runs(self, run):
        return self.in_line(run * self.members + self.member)

    def in_line(self, z):
        return {"grp": self.grp, "dev": z}

    def greet(self):
        barrier = pltpu.get_barrier_semaphore()

        def signal(device):
            pl.semaphore_signal(barrier, inc=1, device_id=device, device_id_type=MESH)

        signal(self.sibling())

        @pl.loop(0, self.planes - 1)
        def _(i):
            signal(self.in_plane(self.plane_partner(i)))

        for i in range(1, self.members):
            signal(self.in_run(self.member_partner(i)))
        for i in range(1, self.runs):
            signal(self.across_runs(self.run_partner(i)))

    def meet(self):
        partners = 1 + self.planes - 1 + self.members - 1 + self.runs - 1
        pl.semaphore_wait(pltpu.get_barrier_semaphore(), partners)


def remote(src, dst, send, recv, device):
    return pltpu.make_async_remote_copy(
        src_ref=src, dst_ref=dst, send_sem=send, recv_sem=recv,
        device_id=device, device_id_type=MESH,
    )


def await_bytes(like, sem):
    pltpu.make_async_copy(like, like, sem).wait()


class AllSum:
    def __init__(self, place, refs):
        self.at = place
        (self.x, self.out, self.pair_buf, self.plane_buf, self.acc, self.z_src, self.z_buf,
         self.z_mid, self.z_all, self.recv, self.send) = refs
        self.chunks, self.half, self.cols = self.pair_buf.shape
        self.part = self.half // place.planes
        self.lane_tiles = self.cols // LANES
        self.per_z = self.part * self.lane_tiles // place.members

    def part_rows(self, c, core, g):
        return pl.ds(pl.multiple_of((2 * c + core) * self.half + g * self.part, 8), self.part)

    def half_rows(self, c, core):
        return pl.ds(pl.multiple_of((2 * c + core) * self.half, 8), self.half)

    def pair(self, c):
        at = self.at
        remote(
            self.x.at[self.half_rows(c, 1 - at.core)], self.pair_buf.at[c],
            self.send.at[0], self.recv.at[0, c], at.sibling(),
        ).start()

    def plane(self, c):
        at = self.at
        await_bytes(self.pair_buf.at[c], self.recv.at[0, c])
        self.pair_buf[c] = self.pair_buf[c] + self.x[self.half_rows(c, at.core)]

        @pl.loop(0, at.planes - 1)
        def _(i):
            g = at.plane_partner(i)
            rows = pl.ds(pl.multiple_of(g * self.part, 8), self.part)
            remote(
                self.pair_buf.at[c, rows], self.plane_buf.at[c, i],
                self.send.at[1], self.recv.at[1, c], at.in_plane(g),
            ).start()

    def line(self, c):
        at = self.at
        await_bytes(self.plane_buf.at[c], self.recv.at[1, c])
        rows = pl.ds(pl.multiple_of(at.xy * self.part, 8), self.part)
        total = self.pair_buf[c, rows]
        for i in range(at.planes - 1):
            total = total + self.plane_buf[c, i]
        self.acc[...] = total
        for s in range(self.part):
            for l in range(self.lane_tiles):
                r = s * self.lane_tiles + l
                self.z_src[c, r // self.per_z, r % self.per_z] = self.acc[
                    s : s + 1, l * LANES : (l + 1) * LANES
                ]

        for i in range(1, at.members):
            member = at.member_partner(i)
            remote(
                self.z_src.at[c, member], self.z_buf.at[c, i - 1],
                self.send.at[2], self.recv.at[2, c], at.in_run(member),
            ).start()

    def line_across(self, c):
        at = self.at
        await_bytes(self.z_buf.at[c], self.recv.at[2, c])
        total = self.z_src[c, at.member]
        for i in range(at.members - 1):
            total = total + self.z_buf[c, i]
        self.z_mid[c, at.run] = total
        for i in range(1, at.runs):
            block = self.z_mid.at[c, at.run]
            remote(
                block, block, self.send.at[3], self.recv.at[3, c],
                at.across_runs(at.run_partner(i)),
            ).start()

    def line_back(self, c):
        at = self.at
        await_bytes(self.z_mid.at[c, pl.ds(0, at.runs - 1)], self.recv.at[3, c])
        total = self.z_mid[c, 0]
        for i in range(1, at.runs):
            total = total + self.z_mid[c, i]
        self.z_all[c, at.member] = total
        for i in range(1, at.members):
            block = self.z_all.at[c, at.member]
            remote(
                block, block, self.send.at[6], self.recv.at[6, c],
                at.in_run(at.member_partner(i)),
            ).start()

    def plane_back(self, c):
        at = self.at
        await_bytes(self.z_buf.at[c], self.recv.at[6, c])
        for s in range(self.part):
            for l in range(self.lane_tiles):
                r = s * self.lane_tiles + l
                self.acc[s : s + 1, l * LANES : (l + 1) * LANES] = self.z_all[
                    c, r // self.per_z, r % self.per_z
                ]
        own = self.part_rows(c, at.core, at.xy)
        self.out[own] = self.acc[...]

        @pl.loop(0, at.planes - 1)
        def _(i):
            block = self.out.at[own]
            remote(
                block, block, self.send.at[4], self.recv.at[4, c],
                at.in_plane(at.plane_partner(i)),
            ).start()

    def pair_back(self, c):
        at = self.at
        await_bytes(self.plane_buf.at[c], self.recv.at[4, c])
        block = self.out.at[self.half_rows(c, at.core)]
        remote(block, block, self.send.at[5], self.recv.at[5, c], at.sibling()).start()

    def arrive(self, c):
        await_bytes(self.pair_buf.at[c], self.recv.at[5, c])

    def drain(self):
        across = self.z_mid.at[:, pl.ds(0, self.at.runs - 1)]
        for k, like in enumerate(
            (self.pair_buf, self.plane_buf, self.z_buf, across, self.plane_buf, self.pair_buf,
             self.z_buf)
        ):
            await_bytes(like, self.send.at[k])


def all_sum_scratch(chunks, rows, cols, nx, ny, nz):
    planes = nx * ny
    part = rows // (2 * planes)
    members, runs = line_shape(nz)
    per_z = part * (cols // LANES) // members
    return [
        pltpu.VMEM((chunks * rows, cols), jnp.float32),
        pltpu.VMEM((chunks * rows, cols), jnp.float32),
        pltpu.VMEM((chunks, rows // 2, cols), jnp.float32),
        pltpu.VMEM((chunks, planes - 1, part, cols), jnp.float32),
        pltpu.VMEM((part, cols), jnp.float32),
        pltpu.VMEM((chunks, members, per_z, 1, LANES), jnp.float32),
        pltpu.VMEM((chunks, members - 1, per_z, 1, LANES), jnp.float32),
        pltpu.VMEM((chunks, runs, per_z, 1, LANES), jnp.float32),
        pltpu.VMEM((chunks, members, per_z, 1, LANES), jnp.float32),
        pltpu.SemaphoreType.DMA((7, chunks)),
        pltpu.SemaphoreType.DMA((7,)),
    ]


def split(value):
    hi = value.astype(jnp.bfloat16)
    return hi, (value - hi.astype(jnp.float32)).astype(jnp.bfloat16)


def dot(a, b, dims):
    return lax.dot_general(
        a, b, dimension_numbers=(dims, ((), ())), preferred_element_type=jnp.float32
    )


def newton_schulz(cross, q, p_hi, p_lo, g_hi, g_lo):
    width = q.shape[0]
    tile = 256
    total = jnp.sum(cross[...] * cross[...], keepdims=True)
    q[...] = cross[...] / (2.0 * jnp.sqrt((total + 1e-06) / width))

    def times(a, b_hi, b_lo, dims):
        return dot(a[0], b_hi, dims) + (dot(a[0], b_lo, dims) + dot(a[1], b_hi, dims))

    @pl.loop(0, NS_STEPS)
    def _(step):
        hi, lo = split(q[...])
        p_hi[...] = hi
        p_lo[...] = lo
        for r in range(0, width, tile):
            band = slice(r, r + tile)
            for c in range(r, width, tile):
                other = slice(c, c + tile)
                gram = times((p_hi[band], p_lo[band]), p_hi[other], p_lo[other], ((1,), (1,)))
                g_hi[band, other], g_lo[band, other] = split(gram)
                if c > r:
                    g_hi[other, band], g_lo[other, band] = split(gram.T)
        for r in range(0, width, tile):
            band = slice(r, r + tile)
            cubic = times((g_hi[band], g_lo[band]), p_hi[...], p_lo[...], ((1,), (0,)))
            q[band] = 1.5 * q[band] - 0.5 * cubic


def kernel(
    nx, ny, nz, emb, ids_t, rot_out, last_out, counts,
    *scratch,
):
    first_refs, cross_refs, last_refs = scratch[0:11], scratch[11:22], scratch[22:32]
    last_refs = (last_refs[0], last_out, *last_refs[1:])
    emb_t, books, recon_t, p_hi, p_lo, g_hi, g_lo, polar, rot, rot_t = scratch[32:]
    rows = emb.shape[0]
    width = emb.shape[1]
    place = Place(nx, ny, nz)
    place.greet()
    first = AllSum(place, first_refs)
    cross = AllSum(place, cross_refs)
    last = AllSum(place, last_refs)
    subs = 24
    top = lax.broadcasted_iota(jnp.int32, (2 * SUBW, rows), 0) < SUBW
    first_eight = lax.broadcasted_iota(jnp.int32, (2 * SUBW, K), 0) < SUBW
    codes = lax.broadcasted_iota(jnp.int32, (K, rows), 0).astype(jnp.float32).astype(jnp.bfloat16)
    one, zero = jnp.array(1, jnp.bfloat16), jnp.array(0, jnp.bfloat16)

    def selector(m):
        return jnp.where(ids_t[pl.ds(m, 1), :].astype(jnp.float32).astype(jnp.bfloat16) == codes, one, zero)

    def pair_rows(m):
        return pl.ds(pl.multiple_of(m * SUBW, 16), 2 * SUBW)

    def first_sums(t):
        base = t * CHUNK

        @pl.loop(0, 2)
        def _(u):
            for s in range(0, subs // 2, 2):
                m = u * (subs // 2) + s
                values = emb_t[pair_rows(t * subs + m), :]
                both = dot(jnp.where(top, values, one), selector(t * subs + m), ((1,), (1,)))
                at = pl.ds(pl.multiple_of(base + m * SUBW, 8), SUBW)
                first.x[at, :] = both[:SUBW]
                first.x[pl.ds(base + subs * SUBW + m, 1), :] = both[SUBW : SUBW + 1]
                both = dot(jnp.where(top, one, values), selector(t * subs + m + 1), ((1,), (1,)))
                at = pl.ds(pl.multiple_of(base + m * SUBW + SUBW, 8), SUBW)
                first.x[at, :] = both[SUBW:]
                first.x[pl.ds(base + subs * SUBW + m + 1, 1), :] = both[:1]

        used = subs * (SUBW + 1)
        first.x[base + used : base + CHUNK, :] = jnp.zeros((CHUNK - used, K), jnp.float32)

    def first_books(t):
        base = t * CHUNK
        tally = base + subs * SUBW
        counts[t * subs : (t + 1) * subs, :] = first.out[tally : tally + subs, :] + 1.0
        for m in range(0, subs, 2):
            g = t * subs + m
            divisor = jnp.where(first_eight, counts[g : g + 1, :], counts[g + 1 : g + 2, :])
            sums = first.out[base + m * SUBW : base + (m + 2) * SUBW, :]
            books[g * SUBW : (g + 2) * SUBW, :] = (sums / divisor).astype(jnp.bfloat16)

        @pl.loop(0, subs // 8)
        def _(u):
            for s in range(0, 8, 2):
                m = t * subs + u * 8 + s
                book = books[pair_rows(m), :]
                even = dot(book, selector(m), ((1,), (0,)))
                odd = dot(book, selector(m + 1), ((1,), (0,)))
                recon_t[pair_rows(m), :] = jnp.where(top, even, odd).astype(jnp.bfloat16)

    def cross_rows(j):
        band = slice(j * CHUNK, (j + 1) * CHUNK)
        cross.x[band, :] = dot(recon_t[band, :], emb[...], ((1,), (0,)))

    def last_sums(j):
        band = slice(j * CHUNK, (j + 1) * CHUNK)
        rot_t[...] = dot(p_hi[band, :], emb_t[...], ((1,), (0,))).astype(jnp.bfloat16)

        @pl.loop(0, 2)
        def _(u):
            for s in range(0, CHUNK // SUBW // 2, 2):
                m = u * (CHUNK // SUBW // 2) + s
                values = rot_t[pair_rows(m), :]
                base = j * CHUNK // SUBW
                even = dot(values, selector(base + m), ((1,), (1,)))
                odd = dot(values, selector(base + m + 1), ((1,), (1,)))
                at = pl.ds(pl.multiple_of(j * CHUNK + m * SUBW, 8), SUBW)
                last.x[at, :] = even[:SUBW]
                at = pl.ds(pl.multiple_of(j * CHUNK + m * SUBW + SUBW, 8), SUBW)
                last.x[at, :] = odd[SUBW:]

    def turn(t):
        band = slice(t * CHUNK, (t + 1) * CHUNK)
        emb_t[band, :] = emb[:, band].T

    turn(0)
    first_sums(0)
    turn(1)
    place.meet()
    first.pair(0)
    first_sums(1)
    first.pair(1)
    first.plane(0)
    turn(2)
    first_sums(2)
    first.pair(2)
    first.plane(1)
    first_sums(3)
    first.pair(3)
    first.plane(2)
    first.line(0)
    first.plane(3)
    for t in range(1, FIRST_CHUNKS):
        first.line(t)
    for t in range(FIRST_CHUNKS):
        first.line_across(t)
    for t in range(FIRST_CHUNKS):
        first.line_back(t)
    for t in range(FIRST_CHUNKS):
        first.plane_back(t)
    first.pair_back(0)
    first.pair_back(1)
    first.arrive(0)
    first_books(0)
    first.pair_back(2)
    first.arrive(1)
    first_books(1)
    cross_rows(0)
    cross.pair(0)
    first.pair_back(3)
    first.arrive(2)
    first_books(2)
    cross_rows(1)
    cross.pair(1)
    cross.plane(0)
    first.arrive(3)
    first_books(3)
    cross_rows(2)
    cross.pair(2)
    cross.plane(1)
    cross.line(0)
    cross.plane(2)
    cross.line(1)
    cross.line(2)
    for stage in (cross.line_across, cross.line_back, cross.plane_back, cross.pair_back, cross.arrive):
        for t in range(CROSS_CHUNKS):
            stage(t)

    newton_schulz(cross.out, polar, p_hi, p_lo, g_hi, g_lo)
    p_hi[...] = polar[...].astype(jnp.bfloat16)
    last_sums(0)
    last.pair(0)
    last_sums(1)
    last.pair(1)
    last.plane(0)
    last_sums(2)
    last.pair(2)
    last.plane(1)
    last.line(0)
    last.plane(2)
    last.line(1)
    last.line(2)
    rot[...] = polar[...].T
    share = width // nz
    rot_out[...] = rot[pl.ds(pl.multiple_of(place.z * share, 8), share), :]
    for stage in (last.line_across, last.line_back, last.plane_back, last.pair_back, last.arrive):
        for t in range(LAST_CHUNKS):
            stage(t)
    first.drain()
    cross.drain()
    last.drain()


def finish(sums, counts, rot, rot_out, books_out):
    rot_out[...] = rot[...]
    for m in range(counts.shape[0]):
        at = slice(m * SUBW, (m + 1) * SUBW)
        books_out[at, :] = sums[at, :] / counts[m : m + 1, :]


def on_device(nz, torus, embeddings, codeword_ids):
    nx, ny = torus
    rows, width = embeddings.shape
    vmem = pl.BlockSpec(memory_space=pltpu.VMEM)
    bf16 = jnp.bfloat16
    square = pltpu.VMEM((width, width), bf16)
    subspaces = codeword_ids.shape[1]
    last_scratch = all_sum_scratch(LAST_CHUNKS, CHUNK, K, nx, ny, nz)
    rotation_shape = jax.ShapeDtypeStruct((width // nz, width), jnp.float32)
    books_shape = jax.ShapeDtypeStruct((width, K), jnp.float32)
    rotation, sums, counts = pl.pallas_call(
        functools.partial(kernel, nx, ny, nz),
        out_shape=(
            rotation_shape, books_shape, jax.ShapeDtypeStruct((subspaces, K), jnp.float32),
        ),
        in_specs=[vmem] * 2,
        out_specs=(vmem, vmem, vmem),
        scratch_shapes=[
            *all_sum_scratch(FIRST_CHUNKS, CHUNK, K, nx, ny, nz),
            *all_sum_scratch(CROSS_CHUNKS, CHUNK, width, nx, ny, nz),
            last_scratch[0],
            *last_scratch[2:],
            pltpu.VMEM((width, rows), bf16),
            pltpu.VMEM((width, K), bf16),
            pltpu.VMEM((width, rows), bf16),
            square, square, square, square,
            pltpu.VMEM((width, width), jnp.float32),
            pltpu.VMEM((width, width), jnp.float32),
            pltpu.VMEM((CHUNK, rows), bf16),
        ],
        compiler_params=pltpu.CompilerParams(
            collective_id=1, has_side_effects=True, vmem_limit_bytes=40 << 20
        ),
        cost_estimate=pl.CostEstimate(
            flops=60 * width**3, bytes_accessed=8 * width * width, transcendentals=0
        ),
    )(embeddings, codeword_ids.T)
    rotation, books = pl.pallas_call(
        finish,
        out_shape=(rotation_shape, books_shape),
        in_specs=[vmem] * 3,
        out_specs=(vmem, vmem),
        compiler_params=pltpu.CompilerParams(vmem_limit_bytes=8 << 20),
    )(sums, counts, rotation)
    return rotation, books.reshape(subspaces, SUBW, K)


def solution(mesh, torus=TORUS):
    return jax.shard_map(
        functools.partial(on_device, mesh.shape["dev"], torus),
        mesh=mesh,
        in_specs=(P(("grp", "dev"), None), P(("grp", "dev"), None)),
        out_specs=(P("dev", None), P()),
        check_vma=False,
    )
```

```python
import functools

import jax
import jax.numpy as jnp
from jax import lax
from jax.experimental import pallas as pl
from jax.experimental.pallas import tpu as pltpu
from jax.sharding import PartitionSpec as P

K = 256
NS_STEPS = 5
LANES = 128
MESH = pl.DeviceIdType.MESH
TORUS = (4, 4)
SUBW = 8
FIRST_CHUNKS = 2
CROSS_CHUNKS = 3
LAST_CHUNKS = 3
CHUNK = 256
CHUNK_SUBS = 24
BAND = 128


def line_shape(nz):
    members = 4 if nz % 16 == 0 else nz // 2
    return members, nz // members


class Place:
    def __init__(self, nx, ny, nz):
        self.nx, self.ny, self.nz, self.planes = nx, ny, nz, nx * ny
        self.grp, self.z = lax.axis_index("grp"), lax.axis_index("dev")
        self.core, self.xy = lax.rem(self.grp, 2), lax.div(self.grp, 2)
        self.x, self.y = lax.div(self.xy, ny), lax.rem(self.xy, ny)
        self.members, self.runs = line_shape(nz)
        self.run, self.member = lax.div(self.z, self.members), lax.rem(self.z, self.members)

    def sibling(self):
        return {"grp": self.xy * 2 + 1 - self.core, "dev": self.z}

    def plane_partner(self, i):
        nx, ny = self.nx, self.ny
        own = (nx - nx // 2) % nx * ny + (ny - ny // 2) % ny
        i = jnp.where(i >= own, i + 1, i)
        dx, dy = nx // 2 + lax.div(i, ny), ny // 2 + lax.rem(i, ny)
        return lax.rem(self.x + dx, nx) * ny + lax.rem(self.y + dy, ny)

    def in_plane(self, g):
        return {"grp": g * 2 + self.core, "dev": self.z}

    def member_partner(self, i):
        return lax.rem(self.member + i, self.members)

    def run_partner(self, i):
        return lax.rem(self.run + i, self.runs)

    def in_run(self, member):
        return self.in_line(self.run * self.members + member)

    def across_runs(self, run):
        return self.in_line(run * self.members + self.member)

    def in_line(self, z):
        return {"grp": self.grp, "dev": z}

    def greet(self):
        barrier = pltpu.get_barrier_semaphore()

        def signal(device):
            pl.semaphore_signal(barrier, inc=1, device_id=device, device_id_type=MESH)

        signal(self.sibling())

        @pl.loop(0, self.planes - 1)
        def _(i):
            signal(self.in_plane(self.plane_partner(i)))

        for i in range(1, self.members):
            signal(self.in_run(self.member_partner(i)))
        for i in range(1, self.runs):
            signal(self.across_runs(self.run_partner(i)))

    def meet(self):
        partners = 1 + self.planes - 1 + self.members - 1 + self.runs - 1
        pl.semaphore_wait(pltpu.get_barrier_semaphore(), partners)


def remote(src, dst, send, recv, device):
    return pltpu.make_async_remote_copy(
        src_ref=src, dst_ref=dst, send_sem=send, recv_sem=recv,
        device_id=device, device_id_type=MESH,
    )


def await_bytes(like, sem):
    pltpu.make_async_copy(like, like, sem).wait()


class AllSum:
    def __init__(self, place, refs):
        self.at = place
        (self.x, self.out, self.plane_buf, self.acc, self.z_src, self.z_buf,
         self.z_mid, self.z_all, self.recv, self.send) = refs
        self.chunks, _, self.part, self.cols = self.plane_buf.shape
        self.rows = self.part * place.planes
        self.shared = self.out.shape[0] > self.x.shape[0]
        self.lane_tiles = self.cols // LANES
        self.per_z = self.part * self.lane_tiles // place.members

    def out_rows(self, c, g, rows):
        start = c * self.rows + g * self.part
        if self.shared:
            start = start + self.at.core * (self.chunks * self.rows)
        return pl.ds(pl.multiple_of(start, 8), rows)

    def x_rows(self, c, g):
        return pl.ds(pl.multiple_of(c * self.rows + g * self.part, 8), self.part)

    def plane(self, c):
        at = self.at

        @pl.loop(0, at.planes - 1)
        def _(i):
            g = at.plane_partner(i)
            remote(
                self.x.at[self.x_rows(c, g)], self.plane_buf.at[c, i],
                self.send.at[1], self.recv.at[1, c], at.in_plane(g),
            ).start()

    def line(self, c):
        at = self.at
        await_bytes(self.plane_buf.at[c], self.recv.at[1, c])
        total = self.x[self.x_rows(c, at.xy)]
        for i in range(at.planes - 1):
            total = total + self.plane_buf[c, i]
        self.acc[...] = total
        for s in range(self.part):
            for l in range(self.lane_tiles):
                r = s * self.lane_tiles + l
                self.z_src[c, r // self.per_z, r % self.per_z] = self.acc[
                    s : s + 1, l * LANES : (l + 1) * LANES
                ]

        for i in range(1, at.members):
            member = at.member_partner(i)
            remote(
                self.z_src.at[c, member], self.z_buf.at[c, i - 1],
                self.send.at[2], self.recv.at[2, c], at.in_run(member),
            ).start()

    def line_across(self, c):
        at = self.at
        await_bytes(self.z_buf.at[c], self.recv.at[2, c])
        total = self.z_src[c, at.member]
        for i in range(at.members - 1):
            total = total + self.z_buf[c, i]
        self.z_mid[c, at.run] = total
        for i in range(1, at.runs):
            block = self.z_mid.at[c, at.run]
            remote(
                block, block, self.send.at[3], self.recv.at[3, c],
                at.across_runs(at.run_partner(i)),
            ).start()

    def line_back(self, c):
        at = self.at
        await_bytes(self.z_mid.at[c, pl.ds(0, at.runs - 1)], self.recv.at[3, c])
        total = self.z_mid[c, 0]
        for i in range(1, at.runs):
            total = total + self.z_mid[c, i]
        self.z_all[c, at.member] = total
        for i in range(1, at.members):
            block = self.z_all.at[c, at.member]
            remote(
                block, block, self.send.at[6], self.recv.at[6, c],
                at.in_run(at.member_partner(i)),
            ).start()

    def plane_back(self, c):
        at = self.at
        await_bytes(self.z_buf.at[c], self.recv.at[6, c])
        for s in range(self.part):
            for l in range(self.lane_tiles):
                r = s * self.lane_tiles + l
                self.acc[s : s + 1, l * LANES : (l + 1) * LANES] = self.z_all[
                    c, r // self.per_z, r % self.per_z
                ]
        own = self.out_rows(c, at.xy, self.part)
        self.out[own] = self.acc[...]

        @pl.loop(0, at.planes - 1)
        def _(i):
            block = self.out.at[own]
            remote(
                block, block, self.send.at[4], self.recv.at[4, c],
                at.in_plane(at.plane_partner(i)),
            ).start()

    def pair_back(self, c):
        await_bytes(self.plane_buf.at[c], self.recv.at[4, c])
        if self.shared:
            block = self.out.at[self.out_rows(c, 0, self.rows)]
            remote(block, block, self.send.at[5], self.recv.at[5, c], self.at.sibling()).start()

    def arrive(self, c):
        await_bytes(self.x.at[pl.ds(c * self.rows, self.rows)], self.recv.at[5, c])

    def drain(self):
        across = self.z_mid.at[:, pl.ds(0, self.at.runs - 1)]
        waits = [(1, self.plane_buf), (2, self.z_buf), (3, across), (4, self.plane_buf), (6, self.z_buf)]
        if self.shared:
            waits.append((5, self.x))
        for k, like in waits:
            await_bytes(like, self.send.at[k])


def all_sum_scratch(chunks, rows, cols, nx, ny, nz, shared):
    planes = nx * ny
    part = rows // planes
    members, runs = line_shape(nz)
    per_z = part * (cols // LANES) // members
    return [
        pltpu.VMEM((chunks * rows, cols), jnp.float32),
        pltpu.VMEM((chunks * rows * (2 if shared else 1), cols), jnp.float32),
        pltpu.VMEM((chunks, planes - 1, part, cols), jnp.float32),
        pltpu.VMEM((part, cols), jnp.float32),
        pltpu.VMEM((chunks, members, per_z, 1, LANES), jnp.float32),
        pltpu.VMEM((chunks, members - 1, per_z, 1, LANES), jnp.float32),
        pltpu.VMEM((chunks, runs, per_z, 1, LANES), jnp.float32),
        pltpu.VMEM((chunks, members, per_z, 1, LANES), jnp.float32),
        pltpu.SemaphoreType.DMA((7, chunks)),
        pltpu.SemaphoreType.DMA((7,)),
    ]


def split(value):
    hi = value.astype(jnp.bfloat16)
    return hi, (value - hi.astype(jnp.float32)).astype(jnp.bfloat16)


def dot(a, b, dims):
    return lax.dot_general(
        a, b, dimension_numbers=(dims, ((), ())), preferred_element_type=jnp.float32
    )


def newton_schulz(cross, q, p_hi, p_lo, g_hi, g_lo):
    width = q.shape[0]
    tile = 256
    total = jnp.sum(cross[...] * cross[...], keepdims=True)
    q[...] = cross[...] / (2.0 * jnp.sqrt((total + 1e-06) / width))

    def times(a, b_hi, b_lo, dims):
        return dot(a[0], b_hi, dims) + (dot(a[0], b_lo, dims) + dot(a[1], b_hi, dims))

    @pl.loop(0, NS_STEPS)
    def _(step):
        hi, lo = split(q[...])
        p_hi[...] = hi
        p_lo[...] = lo
        for r in range(0, width, tile):
            band = slice(r, r + tile)
            for c in range(r, width, tile):
                other = slice(c, c + tile)
                gram = times((p_hi[band], p_lo[band]), p_hi[other], p_lo[other], ((1,), (1,)))
                g_hi[band, other], g_lo[band, other] = split(gram)
                if c > r:
                    g_hi[other, band], g_lo[other, band] = split(gram.T)
        for r in range(0, width, tile):
            band = slice(r, r + tile)
            cubic = times((g_hi[band], g_lo[band]), p_hi[...], p_lo[...], ((1,), (0,)))
            q[band] = 1.5 * q[band] - 0.5 * cubic


def kernel(
    nx, ny, nz, emb, ids_t, rot_out, last_out, counts,
    *scratch,
):
    first_refs, cross_refs, last_refs = scratch[0:10], scratch[10:20], scratch[20:29]
    last_refs = (last_refs[0], last_out, *last_refs[1:])
    (emb_all, emb_t, ids_all, books, recon_t, p_hi, p_lo, g_hi, g_lo, polar, rot, rot_t,
     swap_recv, swap_send) = scratch[29:]
    rows, width = emb.shape
    half = width // 2
    subs = half // SUBW
    place = Place(nx, ny, nz)
    place.greet()
    first = AllSum(place, first_refs)
    cross = AllSum(place, cross_refs)
    last = AllSum(place, last_refs)
    both_rows = 2 * rows
    bf16 = jnp.bfloat16
    top = lax.broadcasted_iota(jnp.int32, (2 * SUBW, both_rows), 0) < SUBW
    first_eight = lax.broadcasted_iota(jnp.int32, (2 * SUBW, K), 0) < SUBW
    codes = lax.broadcasted_iota(jnp.int32, (K, both_rows), 0).astype(jnp.float32).astype(bf16)
    one, zero = jnp.array(1, bf16), jnp.array(0, bf16)
    mine, other = slice(0, rows), slice(rows, both_rows)

    def half_of(core, size):
        return pl.ds(pl.multiple_of(core * size, size), size)

    def selector(m, cols):
        ids = ids_all[pl.ds(m, 1), cols].astype(jnp.float32).astype(bf16)
        return jnp.where(ids == codes[:, cols], one, zero)

    def pair_rows(m):
        return pl.ds(pl.multiple_of(m * SUBW, 16), 2 * SUBW)

    def swaps():
        core = place.core
        theirs, ours = half_of(1 - core, half), half_of(core, half)
        for k, (src, dst) in enumerate((
            (ids_t.at[half_of(1 - core, subs), :], ids_all.at[:, other]),
            (emb.at[:, theirs], emb_all.at[other, theirs]),
            (emb.at[:, ours], emb_all.at[other, ours]),
        )):
            yield remote(src, dst, swap_send.at[k], swap_recv.at[k], place.sibling())

    def landed(k, ref):
        await_bytes(ref, swap_recv.at[k])

    def first_sums(t, cols, part):
        again = cols is other
        base = t * CHUNK
        per = CHUNK_SUBS // 2

        def put(at, value):
            first.x[at, :] = first.x[at, :] + value if again else value

        @pl.loop(part[0], part[1])
        def _(u):
            for s in range(0, per, 2):
                m = u * per + s
                values = emb_t[pair_rows(t * CHUNK_SUBS + m), cols]
                even = dot(
                    jnp.where(top[:, cols], values, one), selector(t * CHUNK_SUBS + m, cols), ((1,), (1,))
                )
                odd = dot(
                    jnp.where(top[:, cols], one, values), selector(t * CHUNK_SUBS + m + 1, cols), ((1,), (1,))
                )
                put(pl.ds(pl.multiple_of(base + m * SUBW, 8), SUBW), even[:SUBW])
                put(pl.ds(base + CHUNK_SUBS * SUBW + m, 1), even[SUBW : SUBW + 1])
                put(pl.ds(pl.multiple_of(base + m * SUBW + SUBW, 8), SUBW), odd[SUBW:])
                put(pl.ds(base + CHUNK_SUBS * SUBW + m + 1, 1), odd[:1])

    def clear(t):
        used = CHUNK_SUBS * (SUBW + 1)
        first.x[t * CHUNK + used : (t + 1) * CHUNK, :] = jnp.zeros((CHUNK - used, K), jnp.float32)

    def first_books(t):
        base = t * CHUNK
        tally = base + CHUNK_SUBS * SUBW
        divisors = first.out[tally : tally + CHUNK_SUBS, :] + 1.0
        own = pl.ds(pl.multiple_of(place.core * subs + t * CHUNK_SUBS, 8), CHUNK_SUBS)
        counts[own, :] = divisors
        for m in range(0, CHUNK_SUBS, 2):
            g = t * CHUNK_SUBS + m
            divisor = jnp.where(first_eight, divisors[m : m + 1, :], divisors[m + 1 : m + 2, :])
            sums = first.out[base + m * SUBW : base + (m + 2) * SUBW, :]
            books[g * SUBW : (g + 2) * SUBW, :] = (sums / divisor).astype(bf16)

        @pl.loop(0, CHUNK_SUBS // 8)
        def _(u):
            for s in range(0, 8, 2):
                m = t * CHUNK_SUBS + u * 8 + s
                book = books[pair_rows(m), :]
                even = dot(book, selector(m, slice(None)), ((1,), (0,)))
                odd = dot(book, selector(m + 1, slice(None)), ((1,), (0,)))
                recon_t[pair_rows(m), :] = jnp.where(top, even, odd).astype(bf16)

    def counts_copy():
        block = counts.at[half_of(place.core, subs), :]
        return remote(block, block, swap_send.at[3], swap_recv.at[3], place.sibling())

    def cross_rows(j):
        band = slice(j * BAND, (j + 1) * BAND)
        cross.x[band, :] = dot(recon_t[band, :], emb_all[...], ((1,), (0,)))

    def last_sums(j):
        own = pl.ds(pl.multiple_of(place.core * half + j * BAND, BAND), BAND)
        rot_t[...] = dot(p_hi[own, :], emb_all[...], ((1,), (1,))).astype(bf16)

        @pl.loop(0, 2)
        def _(u):
            per = BAND // SUBW // 2
            for s in range(0, per, 2):
                m = u * per + s
                values = rot_t[pair_rows(m), :]
                base = j * BAND // SUBW
                even = dot(values, selector(base + m, slice(None)), ((1,), (1,)))
                odd = dot(values, selector(base + m + 1, slice(None)), ((1,), (1,)))
                at = pl.ds(pl.multiple_of(j * BAND + m * SUBW, 8), SUBW)
                last.x[at, :] = even[:SUBW]
                at = pl.ds(pl.multiple_of(j * BAND + m * SUBW + SUBW, 8), SUBW)
                last.x[at, :] = odd[SUBW:]

    ids_all[:, mine] = ids_t[half_of(place.core, subs), :]
    emb_t[:, mine] = emb[:, half_of(place.core, half)].T
    for t in range(FIRST_CHUNKS):
        clear(t)
    first_sums(0, mine, (0, 2))
    first_sums(1, mine, (0, 1))
    place.meet()
    for copy in swaps():
        copy.start()
    emb_all[mine, :] = emb[...]
    first_sums(1, mine, (1, 2))
    landed(0, ids_all.at[:, other])
    landed(1, emb_all.at[other, pl.ds(0, half)])
    emb_t[:, other] = emb_all[other, half_of(place.core, half)].T
    first_sums(0, other, (0, 2))
    first.plane(0)
    first_sums(1, other, (0, 2))
    first.plane(1)
    landed(2, emb_all.at[other, pl.ds(0, half)])
    stages = (first.line, first.line_across, first.line_back, first.plane_back)
    for stage in stages:
        for t in range(FIRST_CHUNKS):
            stage(t)
    first.pair_back(0)
    first_books(0)
    cross_rows(0)
    cross.plane(0)
    first.pair_back(1)
    first_books(1)
    cross_rows(1)
    cross.plane(1)
    cross_rows(2)
    cross.plane(2)
    counts_copy().start()
    stages = (
        cross.line, cross.line_across, cross.line_back, cross.plane_back, cross.pair_back,
        cross.arrive,
    )
    for stage in stages:
        for t in range(CROSS_CHUNKS):
            stage(t)

    newton_schulz(cross.out, polar, p_hi, p_lo, g_hi, g_lo)
    p_hi[...] = polar[...].astype(bf16)
    last_sums(0)
    last.plane(0)
    last_sums(1)
    last.plane(1)
    last_sums(2)
    last.plane(2)
    for t in range(LAST_CHUNKS):
        last.line(t)
    rot[...] = polar[...].T
    share = width // nz
    rot_out[...] = rot[pl.ds(pl.multiple_of(place.z * share, 8), share), :]
    stages = (last.line_across, last.line_back, last.plane_back, last.pair_back, last.arrive)
    for stage in stages:
        for t in range(LAST_CHUNKS):
            stage(t)
    counts_copy().wait()
    for copy in swaps():
        copy.wait_send()
    first.drain()
    cross.drain()
    last.drain()


def finish(sums, counts, rot, rot_out, books_out):
    rot_out[...] = rot[...]
    for m in range(counts.shape[0]):
        at = slice(m * SUBW, (m + 1) * SUBW)
        books_out[at, :] = sums[at, :] / counts[m : m + 1, :]


def on_device(nz, torus, embeddings, codeword_ids):
    nx, ny = torus
    rows, width = embeddings.shape
    vmem = pl.BlockSpec(memory_space=pltpu.VMEM)
    bf16 = jnp.bfloat16
    square = pltpu.VMEM((width, width), bf16)
    subspaces = codeword_ids.shape[1]
    last_scratch = all_sum_scratch(LAST_CHUNKS, BAND, K, nx, ny, nz, True)
    half = width // 2
    rotation_shape = jax.ShapeDtypeStruct((width // nz, width), jnp.float32)
    books_shape = jax.ShapeDtypeStruct((width, K), jnp.float32)
    rotation, sums, counts = pl.pallas_call(
        functools.partial(kernel, nx, ny, nz),
        out_shape=(
            rotation_shape, books_shape, jax.ShapeDtypeStruct((subspaces, K), jnp.float32),
        ),
        in_specs=[vmem] * 2,
        out_specs=(vmem, vmem, vmem),
        scratch_shapes=[
            *all_sum_scratch(FIRST_CHUNKS, CHUNK, K, nx, ny, nz, False),
            *all_sum_scratch(CROSS_CHUNKS, BAND, width, nx, ny, nz, True),
            last_scratch[0],
            *last_scratch[2:],
            pltpu.VMEM((2 * rows, width), bf16),
            pltpu.VMEM((half, 2 * rows), bf16),
            pltpu.VMEM((subspaces // 2, 2 * rows), jnp.int32),
            pltpu.VMEM((half, K), bf16),
            pltpu.VMEM((half, 2 * rows), bf16),
            square, square, square, square,
            pltpu.VMEM((width, width), jnp.float32),
            pltpu.VMEM((width, width), jnp.float32),
            pltpu.VMEM((BAND, 2 * rows), bf16),
            pltpu.SemaphoreType.DMA((4,)),
            pltpu.SemaphoreType.DMA((4,)),
        ],
        compiler_params=pltpu.CompilerParams(
            collective_id=1, has_side_effects=True, vmem_limit_bytes=40 << 20
        ),
        cost_estimate=pl.CostEstimate(
            flops=60 * width**3, bytes_accessed=8 * width * width, transcendentals=0
        ),
    )(embeddings, codeword_ids.T)
    rotation, books = pl.pallas_call(
        finish,
        out_shape=(rotation_shape, books_shape),
        in_specs=[vmem] * 3,
        out_specs=(vmem, vmem),
        compiler_params=pltpu.CompilerParams(vmem_limit_bytes=8 << 20),
    )(sums, counts, rotation)
    return rotation, books.reshape(subspaces, SUBW, K)


def solution(mesh, torus=TORUS):
    return jax.shard_map(
        functools.partial(on_device, mesh.shape["dev"], torus),
        mesh=mesh,
        in_specs=(P(("grp", "dev"), None), P(("grp", "dev"), None)),
        out_specs=(P("dev", None), P()),
        check_vma=False,
    )
```

```python
import functools

import jax
import jax.numpy as jnp
from jax import lax
from jax.experimental import pallas as pl
from jax.experimental.pallas import tpu as pltpu
from jax.sharding import PartitionSpec as P

K = 256
NS_STEPS = 5
LANES = 128
MESH = pl.DeviceIdType.MESH
TORUS = (4, 4)
SUBW = 8
FIRST_CHUNKS = 2
CROSS_CHUNKS = 3
LAST_CHUNKS = 3
CHUNK = 256
CHUNK_SUBS = 24
BAND = 128


def line_shape(nz):
    members = 4 if nz % 16 == 0 else nz // 2
    return members, nz // members


class Place:
    def __init__(self, nx, ny, nz):
        self.nx, self.ny, self.nz, self.planes = nx, ny, nz, nx * ny
        self.grp, self.z = lax.axis_index("grp"), lax.axis_index("dev")
        self.core, self.xy = lax.rem(self.grp, 2), lax.div(self.grp, 2)
        self.x, self.y = lax.div(self.xy, ny), lax.rem(self.xy, ny)
        self.members, self.runs = line_shape(nz)
        self.run, self.member = lax.div(self.z, self.members), lax.rem(self.z, self.members)

    def sibling(self):
        return {"grp": self.xy * 2 + 1 - self.core, "dev": self.z}

    def plane_partner(self, i):
        nx, ny = self.nx, self.ny
        own = (nx - nx // 2) % nx * ny + (ny - ny // 2) % ny
        i = jnp.where(i >= own, i + 1, i)
        dx, dy = nx // 2 + lax.div(i, ny), ny // 2 + lax.rem(i, ny)
        return lax.rem(self.x + dx, nx) * ny + lax.rem(self.y + dy, ny)

    def in_plane(self, g):
        return {"grp": g * 2 + self.core, "dev": self.z}

    def member_partner(self, i):
        return lax.rem(self.member + i, self.members)

    def run_partner(self, i):
        return lax.rem(self.run + i, self.runs)

    def in_run(self, member):
        return self.in_line(self.run * self.members + member)

    def across_runs(self, run):
        return self.in_line(run * self.members + self.member)

    def in_line(self, z):
        return {"grp": self.grp, "dev": z}

    def greet(self):
        barrier = pltpu.get_barrier_semaphore()

        def signal(device):
            pl.semaphore_signal(barrier, inc=1, device_id=device, device_id_type=MESH)

        signal(self.sibling())

        @pl.loop(0, self.planes - 1)
        def _(i):
            signal(self.in_plane(self.plane_partner(i)))

        for i in range(1, self.members):
            signal(self.in_run(self.member_partner(i)))
        for i in range(1, self.runs):
            signal(self.across_runs(self.run_partner(i)))

    def meet(self):
        partners = 1 + self.planes - 1 + self.members - 1 + self.runs - 1
        pl.semaphore_wait(pltpu.get_barrier_semaphore(), partners)


def remote(src, dst, send, recv, device):
    return pltpu.make_async_remote_copy(
        src_ref=src, dst_ref=dst, send_sem=send, recv_sem=recv,
        device_id=device, device_id_type=MESH,
    )


def await_bytes(like, sem):
    pltpu.make_async_copy(like, like, sem).wait()


class AllSum:
    def __init__(self, place, refs):
        self.at = place
        (self.x, self.out, self.plane_buf, self.acc, self.z_src, self.z_buf,
         self.z_mid, self.z_all, self.recv, self.send) = refs
        self.chunks, _, self.part, self.cols = self.plane_buf.shape
        self.rows = self.part * place.planes
        self.shared = self.out.shape[0] > self.x.shape[0]
        self.lane_tiles = self.cols // LANES
        self.per_z = self.part * self.lane_tiles // place.members

    def out_rows(self, c, g, rows):
        start = c * self.rows + g * self.part
        if self.shared:
            start = start + self.at.core * (self.chunks * self.rows)
        return pl.ds(pl.multiple_of(start, 8), rows)

    def x_rows(self, c, g):
        return pl.ds(pl.multiple_of(c * self.rows + g * self.part, 8), self.part)

    def plane(self, c):
        at = self.at

        @pl.loop(0, at.planes - 1)
        def _(i):
            g = at.plane_partner(i)
            remote(
                self.x.at[self.x_rows(c, g)], self.plane_buf.at[c, i],
                self.send.at[1], self.recv.at[1, c], at.in_plane(g),
            ).start()

    def line(self, c):
        at = self.at
        await_bytes(self.plane_buf.at[c], self.recv.at[1, c])
        total = self.x[self.x_rows(c, at.xy)]
        for i in range(at.planes - 1):
            total = total + self.plane_buf[c, i]
        self.acc[...] = total
        for s in range(self.part):
            for l in range(self.lane_tiles):
                r = s * self.lane_tiles + l
                self.z_src[c, r // self.per_z, r % self.per_z] = self.acc[
                    s : s + 1, l * LANES : (l + 1) * LANES
                ]

        for i in range(1, at.members):
            member = at.member_partner(i)
            remote(
                self.z_src.at[c, member], self.z_buf.at[c, i - 1],
                self.send.at[2], self.recv.at[2, c], at.in_run(member),
            ).start()

    def line_across(self, c):
        at = self.at
        await_bytes(self.z_buf.at[c], self.recv.at[2, c])
        total = self.z_src[c, at.member]
        for i in range(at.members - 1):
            total = total + self.z_buf[c, i]
        self.z_mid[c, at.run] = total
        for i in range(1, at.runs):
            block = self.z_mid.at[c, at.run]
            remote(
                block, block, self.send.at[3], self.recv.at[3, c],
                at.across_runs(at.run_partner(i)),
            ).start()

    def line_back(self, c):
        at = self.at
        await_bytes(self.z_mid.at[c, pl.ds(0, at.runs - 1)], self.recv.at[3, c])
        total = self.z_mid[c, 0]
        for i in range(1, at.runs):
            total = total + self.z_mid[c, i]
        self.z_all[c, at.member] = total
        for i in range(1, at.members):
            block = self.z_all.at[c, at.member]
            remote(
                block, block, self.send.at[6], self.recv.at[6, c],
                at.in_run(at.member_partner(i)),
            ).start()

    def plane_back(self, c):
        at = self.at
        await_bytes(self.z_buf.at[c], self.recv.at[6, c])
        for s in range(self.part):
            for l in range(self.lane_tiles):
                r = s * self.lane_tiles + l
                self.acc[s : s + 1, l * LANES : (l + 1) * LANES] = self.z_all[
                    c, r // self.per_z, r % self.per_z
                ]
        own = self.out_rows(c, at.xy, self.part)
        self.out[own] = self.acc[...]

        @pl.loop(0, at.planes - 1)
        def _(i):
            block = self.out.at[own]
            remote(
                block, block, self.send.at[4], self.recv.at[4, c],
                at.in_plane(at.plane_partner(i)),
            ).start()

    def pair_back(self, c):
        await_bytes(self.plane_buf.at[c], self.recv.at[4, c])
        if self.shared:
            block = self.out.at[self.out_rows(c, 0, self.rows)]
            remote(block, block, self.send.at[5], self.recv.at[5, c], self.at.sibling()).start()

    def arrive(self, c):
        await_bytes(self.x.at[pl.ds(c * self.rows, self.rows)], self.recv.at[5, c])

    def drain(self):
        across = self.z_mid.at[:, pl.ds(0, self.at.runs - 1)]
        waits = [(1, self.plane_buf), (2, self.z_buf), (3, across), (4, self.plane_buf), (6, self.z_buf)]
        if self.shared:
            waits.append((5, self.x))
        for k, like in waits:
            await_bytes(like, self.send.at[k])


def all_sum_scratch(chunks, rows, cols, nx, ny, nz, shared):
    planes = nx * ny
    part = rows // planes
    members, runs = line_shape(nz)
    per_z = part * (cols // LANES) // members
    return [
        pltpu.VMEM((chunks * rows, cols), jnp.float32),
        pltpu.VMEM((chunks * rows * (2 if shared else 1), cols), jnp.float32),
        pltpu.VMEM((chunks, planes - 1, part, cols), jnp.float32),
        pltpu.VMEM((part, cols), jnp.float32),
        pltpu.VMEM((chunks, members, per_z, 1, LANES), jnp.float32),
        pltpu.VMEM((chunks, members - 1, per_z, 1, LANES), jnp.float32),
        pltpu.VMEM((chunks, runs, per_z, 1, LANES), jnp.float32),
        pltpu.VMEM((chunks, members, per_z, 1, LANES), jnp.float32),
        pltpu.SemaphoreType.DMA((7, chunks)),
        pltpu.SemaphoreType.DMA((7,)),
    ]


def split(value):
    hi = value.astype(jnp.bfloat16)
    return hi, (value - hi.astype(jnp.float32)).astype(jnp.bfloat16)


def dot(a, b, dims):
    return lax.dot_general(
        a, b, dimension_numbers=(dims, ((), ())), preferred_element_type=jnp.float32
    )


def newton_schulz(cross, q, p_hi, p_lo, g_hi, g_lo):
    width = q.shape[0]
    tile = 256
    total = jnp.sum(cross[...] * cross[...], keepdims=True)
    scale = 2.0 * jnp.sqrt((total + 1e-06) / width)
    for r in range(0, width, tile):
        band = slice(r, r + tile)
        fresh = cross[band, :] / scale
        q[band, :] = fresh
        p_hi[0, band, :], p_lo[0, band, :] = split(fresh)

    def times(a, b_hi, b_lo, dims):
        return dot(a[0], b_hi, dims) + (dot(a[0], b_lo, dims) + dot(a[1], b_hi, dims))

    for step in range(NS_STEPS):
        now = step % 2
        hi, lo = p_hi.at[now], p_lo.at[now]
        for r in range(0, width, tile):
            band = slice(r, r + tile)
            for c in range(r, width, tile):
                other = slice(c, c + tile)
                if c == r:
                    mixed = dot(hi[band, :], lo[band, :], ((1,), (1,)))
                    gram = dot(hi[band, :], hi[band, :], ((1,), (1,))) + (mixed + mixed.T)
                else:
                    gram = times(
                        (hi[band, :], lo[band, :]), hi[other, :], lo[other, :], ((1,), (1,))
                    )
                g_hi[band, other], g_lo[band, other] = split(gram)
                if c > r:
                    g_hi[other, band], g_lo[other, band] = split(gram.T)
        for r in range(0, width, tile):
            band = slice(r, r + tile)
            cubic = times((g_hi[band, :], g_lo[band, :]), hi[...], lo[...], ((1,), (0,)))
            fresh = 1.5 * q[band, :] - 0.5 * cubic
            q[band, :] = fresh
            p_hi[1 - now, band, :], p_lo[1 - now, band, :] = split(fresh)


def kernel(
    nx, ny, nz, emb, ids_t, rot_out, last_out, counts,
    *scratch,
):
    first_refs, cross_refs, last_refs = scratch[0:10], scratch[10:20], scratch[20:29]
    last_refs = (last_refs[0], last_out, *last_refs[1:])
    (emb_all, emb_t, ids_all, books, recon_t, p_hi, p_lo, g_hi, g_lo, polar, rot, rot_t,
     swap_recv, swap_send) = scratch[29:]
    rows, width = emb.shape
    half = width // 2
    subs = half // SUBW
    place = Place(nx, ny, nz)
    place.greet()
    first = AllSum(place, first_refs)
    cross = AllSum(place, cross_refs)
    last = AllSum(place, last_refs)
    both_rows = 2 * rows
    bf16 = jnp.bfloat16
    top = lax.broadcasted_iota(jnp.int32, (2 * SUBW, both_rows), 0) < SUBW
    first_eight = lax.broadcasted_iota(jnp.int32, (2 * SUBW, K), 0) < SUBW
    codes = lax.broadcasted_iota(jnp.int32, (K, both_rows), 0).astype(jnp.float32).astype(bf16)
    one, zero = jnp.array(1, bf16), jnp.array(0, bf16)
    mine, other = slice(0, rows), slice(rows, both_rows)

    def half_of(core, size):
        return pl.ds(pl.multiple_of(core * size, size), size)

    def selector(m, cols):
        ids = ids_all[pl.ds(m, 1), cols].astype(jnp.float32).astype(bf16)
        return jnp.where(ids == codes[:, cols], one, zero)

    def pair_rows(m):
        return pl.ds(pl.multiple_of(m * SUBW, 16), 2 * SUBW)

    def swaps():
        core = place.core
        theirs, ours = half_of(1 - core, half), half_of(core, half)
        for k, (src, dst) in enumerate((
            (ids_t.at[half_of(1 - core, subs), :], ids_all.at[:, other]),
            (emb.at[:, theirs], emb_all.at[other, theirs]),
            (emb.at[:, ours], emb_all.at[other, ours]),
        )):
            yield remote(src, dst, swap_send.at[k], swap_recv.at[k], place.sibling())

    def landed(k, ref):
        await_bytes(ref, swap_recv.at[k])

    def first_sums(t, cols, part):
        again = cols is other
        base = t * CHUNK
        per = CHUNK_SUBS // 2

        def put(at, value):
            first.x[at, :] = first.x[at, :] + value if again else value

        @pl.loop(part[0], part[1])
        def _(u):
            for s in range(0, per, 2):
                m = u * per + s
                values = emb_t[pair_rows(t * CHUNK_SUBS + m), cols]
                even = dot(
                    jnp.where(top[:, cols], values, one), selector(t * CHUNK_SUBS + m, cols), ((1,), (1,))
                )
                odd = dot(
                    jnp.where(top[:, cols], one, values), selector(t * CHUNK_SUBS + m + 1, cols), ((1,), (1,))
                )
                put(pl.ds(pl.multiple_of(base + m * SUBW, 8), SUBW), even[:SUBW])
                put(pl.ds(base + CHUNK_SUBS * SUBW + m, 1), even[SUBW : SUBW + 1])
                put(pl.ds(pl.multiple_of(base + m * SUBW + SUBW, 8), SUBW), odd[SUBW:])
                put(pl.ds(base + CHUNK_SUBS * SUBW + m + 1, 1), odd[:1])

    def clear(t):
        used = CHUNK_SUBS * (SUBW + 1)
        first.x[t * CHUNK + used : (t + 1) * CHUNK, :] = jnp.zeros((CHUNK - used, K), jnp.float32)

    def first_books(t):
        base = t * CHUNK
        tally = base + CHUNK_SUBS * SUBW
        divisors = first.out[tally : tally + CHUNK_SUBS, :] + 1.0
        own = pl.ds(pl.multiple_of(place.core * subs + t * CHUNK_SUBS, 8), CHUNK_SUBS)
        counts[own, :] = divisors
        for m in range(0, CHUNK_SUBS, 2):
            g = t * CHUNK_SUBS + m
            divisor = jnp.where(first_eight, divisors[m : m + 1, :], divisors[m + 1 : m + 2, :])
            sums = first.out[base + m * SUBW : base + (m + 2) * SUBW, :]
            books[g * SUBW : (g + 2) * SUBW, :] = (sums / divisor).astype(bf16)

        @pl.loop(0, CHUNK_SUBS // 8)
        def _(u):
            for s in range(0, 8, 2):
                m = t * CHUNK_SUBS + u * 8 + s
                book = books[pair_rows(m), :]
                even = dot(book, selector(m, slice(None)), ((1,), (0,)))
                odd = dot(book, selector(m + 1, slice(None)), ((1,), (0,)))
                recon_t[pair_rows(m), :] = jnp.where(top, even, odd).astype(bf16)

    def counts_copy():
        block = counts.at[half_of(place.core, subs), :]
        return remote(block, block, swap_send.at[3], swap_recv.at[3], place.sibling())

    def cross_rows(j):
        band = slice(j * BAND, (j + 1) * BAND)
        cross.x[band, :] = dot(recon_t[band, :], emb_all[...], ((1,), (0,)))

    def last_sums(j):
        own = pl.ds(pl.multiple_of(place.core * half + j * BAND, BAND), BAND)
        rot_t[...] = dot(p_hi[NS_STEPS % 2, own, :], emb_all[...], ((1,), (1,))).astype(bf16)

        @pl.loop(0, 2)
        def _(u):
            per = BAND // SUBW // 2
            for s in range(0, per, 2):
                m = u * per + s
                values = rot_t[pair_rows(m), :]
                base = j * BAND // SUBW
                even = dot(values, selector(base + m, slice(None)), ((1,), (1,)))
                odd = dot(values, selector(base + m + 1, slice(None)), ((1,), (1,)))
                at = pl.ds(pl.multiple_of(j * BAND + m * SUBW, 8), SUBW)
                last.x[at, :] = even[:SUBW]
                at = pl.ds(pl.multiple_of(j * BAND + m * SUBW + SUBW, 8), SUBW)
                last.x[at, :] = odd[SUBW:]

    ids_all[:, mine] = ids_t[half_of(place.core, subs), :]
    emb_t[:, mine] = emb[:, half_of(place.core, half)].T
    for t in range(FIRST_CHUNKS):
        clear(t)
    first_sums(0, mine, (0, 2))
    first_sums(1, mine, (0, 1))
    place.meet()
    for copy in swaps():
        copy.start()
    emb_all[mine, :] = emb[...]
    first_sums(1, mine, (1, 2))
    landed(0, ids_all.at[:, other])
    landed(1, emb_all.at[other, pl.ds(0, half)])
    emb_t[:, other] = emb_all[other, half_of(place.core, half)].T
    first_sums(0, other, (0, 2))
    first.plane(0)
    first_sums(1, other, (0, 2))
    first.plane(1)
    landed(2, emb_all.at[other, pl.ds(0, half)])
    stages = (first.line, first.line_across, first.line_back, first.plane_back)
    for stage in stages:
        for t in range(FIRST_CHUNKS):
            stage(t)
    first.pair_back(0)
    first_books(0)
    cross_rows(0)
    cross.plane(0)
    first.pair_back(1)
    first_books(1)
    cross_rows(1)
    cross.plane(1)
    cross_rows(2)
    cross.plane(2)
    counts_copy().start()
    stages = (
        cross.line, cross.line_across, cross.line_back, cross.plane_back, cross.pair_back,
        cross.arrive,
    )
    for stage in stages:
        for t in range(CROSS_CHUNKS):
            stage(t)

    newton_schulz(cross.out, polar, p_hi, p_lo, g_hi, g_lo)
    last_sums(0)
    last.plane(0)
    last_sums(1)
    last.plane(1)
    last_sums(2)
    last.plane(2)
    for t in range(LAST_CHUNKS):
        last.line(t)
    rot[...] = polar[...].T
    share = width // nz
    rot_out[...] = rot[pl.ds(pl.multiple_of(place.z * share, 8), share), :]
    stages = (last.line_across, last.line_back, last.plane_back, last.pair_back, last.arrive)
    for stage in stages:
        for t in range(LAST_CHUNKS):
            stage(t)
    counts_copy().wait()
    for copy in swaps():
        copy.wait_send()
    first.drain()
    cross.drain()
    last.drain()


def finish(sums, counts, rot, rot_out, books_out):
    rot_out[...] = rot[...]
    for m in range(counts.shape[0]):
        at = slice(m * SUBW, (m + 1) * SUBW)
        books_out[at, :] = sums[at, :] / counts[m : m + 1, :]


def on_device(nz, torus, embeddings, codeword_ids):
    nx, ny = torus
    rows, width = embeddings.shape
    vmem = pl.BlockSpec(memory_space=pltpu.VMEM)
    bf16 = jnp.bfloat16
    square = pltpu.VMEM((width, width), bf16)
    subspaces = codeword_ids.shape[1]
    last_scratch = all_sum_scratch(LAST_CHUNKS, BAND, K, nx, ny, nz, True)
    half = width // 2
    rotation_shape = jax.ShapeDtypeStruct((width // nz, width), jnp.float32)
    books_shape = jax.ShapeDtypeStruct((width, K), jnp.float32)
    rotation, sums, counts = pl.pallas_call(
        functools.partial(kernel, nx, ny, nz),
        out_shape=(
            rotation_shape, books_shape, jax.ShapeDtypeStruct((subspaces, K), jnp.float32),
        ),
        in_specs=[vmem] * 2,
        out_specs=(vmem, vmem, vmem),
        scratch_shapes=[
            *all_sum_scratch(FIRST_CHUNKS, CHUNK, K, nx, ny, nz, False),
            *all_sum_scratch(CROSS_CHUNKS, BAND, width, nx, ny, nz, True),
            last_scratch[0],
            *last_scratch[2:],
            pltpu.VMEM((2 * rows, width), bf16),
            pltpu.VMEM((half, 2 * rows), bf16),
            pltpu.VMEM((subspaces // 2, 2 * rows), jnp.int32),
            pltpu.VMEM((half, K), bf16),
            pltpu.VMEM((half, 2 * rows), bf16),
            pltpu.VMEM((2, width, width), bf16),
            pltpu.VMEM((2, width, width), bf16),
            square,
            square,
            pltpu.VMEM((width, width), jnp.float32),
            pltpu.VMEM((width, width), jnp.float32),
            pltpu.VMEM((BAND, 2 * rows), bf16),
            pltpu.SemaphoreType.DMA((4,)),
            pltpu.SemaphoreType.DMA((4,)),
        ],
        compiler_params=pltpu.CompilerParams(
            collective_id=1, has_side_effects=True, vmem_limit_bytes=40 << 20
        ),
        cost_estimate=pl.CostEstimate(
            flops=60 * width**3, bytes_accessed=8 * width * width, transcendentals=0
        ),
    )(embeddings, codeword_ids.T)
    rotation, books = pl.pallas_call(
        finish,
        out_shape=(rotation_shape, books_shape),
        in_specs=[vmem] * 3,
        out_specs=(vmem, vmem),
        compiler_params=pltpu.CompilerParams(vmem_limit_bytes=8 << 20),
    )(sums, counts, rotation)
    return rotation, books.reshape(subspaces, SUBW, K)


def solution(mesh, torus=TORUS):
    return jax.shard_map(
        functools.partial(on_device, mesh.shape["dev"], torus),
        mesh=mesh,
        in_specs=(P(("grp", "dev"), None), P(("grp", "dev"), None)),
        out_specs=(P("dev", None), P()),
        check_vma=False,
    )
```
